256 devices in a mesh: pair: 2 (over core), wide: 32 (over y, x, z_lo), rep: 4 (over z_hi).
Axes of the slice: x: 4, y: 4, z: 8 (z_hi: 4, z_lo: 2; z = z_hi * 2 + z_lo), core: 2. Of those that a mesh axis runs over, the one named last changes fastest.
Arguments:
- tokens: bfloat16 [32768, 2560], P(('pair', 'wide', 'rep')), may hold values from -6 to 6
- out_grad: bfloat16 [32768, 2560], P(('pair', 'wide', 'rep')), may hold values from -1.5 to 1.5
- expert_ids: int32 [32768, 6], P(('pair', 'wide', 'rep')), may hold values from 0 to 159, all different within a row; in each aligned block of 128 rows (0 to 127, 128 to 255, ...) at most 12 rows name the same one
- gate_vals: float32 [32768, 6], P(('pair', 'wide', 'rep')), may hold values from 0.03 to 0.6
- gate_weight: bfloat16 [32, 2560, 768], P('wide', None, 'pair'), may hold values from -0.125 to 0.125
- up_weight: bfloat16 [32, 2560, 768], P('wide', None, 'pair'), may hold values from -0.125 to 0.125
- down_weight: bfloat16 [32, 768, 2560], P('wide', 'pair'), may hold values from -0.21875 to 0.21875
Outputs:
- x_grad: bfloat16 [32768, 2560], P(('pair', 'wide', 'rep'))
- gate_grad: float32 [32, 2560, 768], P('wide', 'rep', 'pair')
- up_grad: float32 [32, 2560, 768], P('wide', 'rep', 'pair')
- down_grad: float32 [32, 768, 2560], P('wide', 'pair', 'rep')
The draws below stay inside these ranges and needn't reach their ends.
Inputs may be any that keep to these rules, and one draw needn't show every extreme that they name: `expert_ids`: each row names 6 different experts; in the 128 rows of one device no expert is named by more than 12 rows.
All inputs are finite; a program needn't handle non-finite values.
Results may differ from the reference program's by a relative error of at most 0.014.
Values may be sent and summed in bfloat16 or wider, within the bound.
No kernel may reach another device: no remote copies, remote signals or barrier semaphores. Data moves between devices by JAX's collectives and lax.ppermute only.
A program may use at most 192 MiB of HBM per device.

```python
import math
import jax
import jax.numpy as jnp
import numpy as np
from jax import lax

D = 2560
FF = 768
EXPERTS = 160
K = 6
WINDOW = 32
TOK_DEV = 128
CAP = 12
TOKENS = 32768


def level_of(stream_key, extent, cuts, low, high):
    factor_of = 1.0
    for axis_at, parts in cuts:
        steps = jax.random.uniform(jax.random.fold_in(jax.random.fold_in(stream_key, 6), axis_at), (parts,), jnp.float32, low / len(cuts), high / len(cuts))
        factor_of = factor_of * jnp.repeat(jnp.exp(steps), extent[axis_at] // parts).reshape((-1,) + (1,) * (len(extent) - 1 - axis_at))
    return factor_of


def shared_out(rng, own, number, rows, amount, top, limit, skew):
    order = jax.random.permutation(rng, amount)
    heavy_load, ordinary = portions_of(amount, rows * top, limit, skew, True), portions_of(amount, rows * top, limit, skew, False)
    places = jnp.arange(amount)

    def named(sizes, turn):
        used = int((sizes > 0).sum())
        fixed = max(1, used // 4)
        moved = fixed + (places - fixed + turn * (used - fixed)) % max(1, amount - fixed)
        return jnp.zeros((amount,), jnp.int32).at[order[jnp.where(places < fixed, places, moved)]].set(jnp.asarray(sizes, jnp.int32))

    sizes = jnp.where(number % 4 == 0, named(heavy_load, number // 4), named(ordinary, number - number // 4 - 1))
    mixed = jax.random.permutation(jax.random.fold_in(own, 3), amount)
    giver, sink = mixed[0:amount // 2 * 2:2], mixed[1:amount // 2 * 2:2]
    margin = jnp.minimum(sizes[giver] - 1, limit - sizes[sink]) // 2
    margin = jnp.where((giver == order[0]) | (sink == order[0]) | (sizes[sink] == 0), 0, jnp.maximum(margin, 0))
    moved = jax.random.randint(jax.random.fold_in(own, 4), (amount // 2,), 0, 1 << 20) % (margin + 1)
    sizes = sizes.at[giver].add(-moved).at[sink].add(moved)
    members = jnp.searchsorted(jnp.cumsum(sizes), jnp.arange(rows * top), side="right").astype(jnp.int32)
    table = members.reshape(top, rows).T
    table = table[jax.random.permutation(jax.random.fold_in(own, 1), rows)]
    turn = jax.random.randint(jax.random.fold_in(own, 2), (rows, 1), 0, top)
    return jnp.take_along_axis(table, (jnp.arange(top)[None, :] + turn) % top, axis=1)


def portions_of(amount, total, most, slope, full):
    weights = [(1 << 20) // math.isqrt(standing ** slope) + 1 for standing in range(1, amount + 1)]
    largest = most if full else min(most, max(-(-total // amount), total * weights[0] // sum(weights)))
    least = 1 if total - largest >= amount - 1 else 0
    holding, rest = [largest] + [least] * (amount - 1), total - largest - least * (amount - 1)
    while rest > 0:
        candidates = [i for i in range(1, amount) if holding[i] < largest] or [i for i in range(1, amount) if holding[i] < most]
        mass, remaining = sum([weights[i] for i in candidates]), rest
        for i in candidates:
            extra = min(most - holding[i], max(1, remaining * weights[i] // mass), rest)
            holding[i] = holding[i] + extra
            rest = rest - extra
    return np.array(holding)


def bell_draw(stream_key, extent, deviation, bound, cuts=(), kind=jnp.bfloat16):
    factor_of = level_of(stream_key, extent, cuts, -0.22, 0.18) if cuts else 1.0
    array = jax.random.normal(stream_key, extent, jnp.float32) * deviation * factor_of
    return jnp.minimum(jnp.maximum(array, -bound), bound).astype(kind)


def setup_inputs(seed: int = 0) -> dict:
    streams_of = jax.random.split(jax.random.key(seed), 8)
    tokens = bell_draw(streams_of[0], (TOKENS, D), 1.0, 6.0, ((0, 256),))
    out_grad = bell_draw(streams_of[1], (TOKENS, D), 0.25, 1.5, ((0, 256),))
    expert_ids_keys = jax.random.split(jax.random.fold_in(streams_of[2], 1), TOKENS // TOK_DEV)
    expert_ids_turns = jax.random.permutation(jax.random.fold_in(streams_of[2], 3), TOKENS // TOK_DEV)
    expert_ids = jax.vmap(lambda own, number: shared_out(jax.random.fold_in(streams_of[2], 2), own, number, TOK_DEV, EXPERTS, K, CAP, 2))(expert_ids_keys, expert_ids_turns).reshape((TOKENS, K))
    gate_vals = jnp.clip(jnp.exp(math.log(0.6) - 2.9957323 * jax.random.uniform(streams_of[3], (TOKENS, K), jnp.float32) ** level_of(streams_of[3], (TOKENS, K), ((0, 256),), -0.2, 0.2)), 0.03, 0.6)
    gate_weight = bell_draw(streams_of[4], (WINDOW, D, FF), D ** -0.5, 0.125, ((0, 32), (2, 2)))
    up_weight = bell_draw(streams_of[5], (WINDOW, D, FF), D ** -0.5, 0.125, ((0, 32), (2, 2)))
    down_weight = bell_draw(streams_of[6], (WINDOW, FF, D), FF ** -0.5, 0.21875, ((0, 32), (1, 2)))
    return {"tokens": tokens, "out_grad": out_grad, "expert_ids": expert_ids, "gate_vals": gate_vals, "gate_weight": gate_weight, "up_weight": up_weight, "down_weight": down_weight}


def slot_tables(expert_ids, gate_vals, window, capacity):
    row_count = expert_ids.shape[0]
    choice_count = expert_ids.shape[1]
    flat_ids = expert_ids.reshape(-1)
    flat_gate = gate_vals.reshape(-1)
    chosen = (flat_ids[:, None] == jnp.arange(window, dtype=jnp.int32)[None, :]).astype(jnp.int32)
    before = jnp.cumsum(chosen, axis=0) - chosen
    position = jnp.sum(before * chosen, axis=1)
    inside = jnp.sum(chosen, axis=1)
    target = jnp.where(inside > 0, flat_ids * capacity + position, -1)
    matches = (jnp.arange(window * capacity, dtype=jnp.int32)[:, None] == target[None, :]).astype(jnp.int32)
    matches = matches.reshape(window * capacity, row_count, choice_count)
    picked = jnp.sum(matches, axis=2)
    weights = jnp.sum(matches.astype(flat_gate.dtype) * gate_vals[None, :, :], axis=2)
    return picked, weights


def silu_parts(preact):
    sigmoid_val = jax.nn.sigmoid(preact)
    return preact * sigmoid_val, sigmoid_val * (1.0 + preact * (1.0 - sigmoid_val))


def reference(tokens, out_grad, expert_ids, gate_vals, gate_weight, up_weight, down_weight):
    block_total = TOKENS // TOK_DEV
    ids_blocks = expert_ids.reshape(block_total, TOK_DEV, K)
    gate_blocks = gate_vals.reshape(block_total, TOK_DEV, K)

    def one_block(pieces):
        picked, weights = slot_tables(pieces[0], pieces[1], WINDOW, CAP)
        token_of = jnp.sum(picked * jnp.arange(TOK_DEV, dtype=jnp.int32)[None, :], axis=1).astype(jnp.int32)
        return token_of, jnp.sum(picked, axis=1).astype(jnp.int32), jnp.sum(weights, axis=1)

    token_of, filled, scales = lax.map(one_block, (ids_blocks, gate_blocks))
    offsets = (jnp.arange(block_total, dtype=jnp.int32) * TOK_DEV)[:, None]
    slot_token = (token_of + offsets).astype(jnp.int32)
    slot_token = slot_token.reshape(block_total, WINDOW, CAP).transpose(1, 0, 2).reshape(WINDOW, block_total * CAP)
    filled = filled.reshape(block_total, WINDOW, CAP).transpose(1, 0, 2).reshape(WINDOW, block_total * CAP)
    scales = scales.reshape(block_total, WINDOW, CAP).transpose(1, 0, 2).reshape(WINDOW, block_total * CAP)

    def expert_step(total, pieces):
        rows_index, rows_filled, rows_scale, w_gate, w_up, w_down = pieces
        keep = rows_filled.astype(jnp.float32)
        expert_in = tokens[rows_index] * keep[:, None].astype(tokens.dtype)
        expert_grad = (rows_scale[:, None] * out_grad[rows_index].astype(jnp.float32)).astype(jnp.bfloat16)
        gate_pre = jnp.dot(expert_in, w_gate, preferred_element_type=jnp.float32)
        up_pre = jnp.dot(expert_in, w_up, preferred_element_type=jnp.float32)
        silu_val, silu_slope = silu_parts(gate_pre)
        hidden_act = (silu_val * up_pre).astype(jnp.bfloat16)
        act_grad = jnp.dot(expert_grad, w_down.T, preferred_element_type=jnp.float32)
        gate_back = (act_grad * up_pre * silu_slope).astype(jnp.bfloat16)
        up_back = (act_grad * silu_val).astype(jnp.bfloat16)
        row_grad = (jnp.dot(gate_back, w_gate.T, preferred_element_type=jnp.float32)
                    + jnp.dot(up_back, w_up.T, preferred_element_type=jnp.float32)).astype(jnp.bfloat16)
        total = total.at[rows_index].add(row_grad.astype(jnp.float32) * keep[:, None])
        grad_gate = jnp.dot(expert_in.T, gate_back, preferred_element_type=jnp.float32)
        grad_up = jnp.dot(expert_in.T, up_back, preferred_element_type=jnp.float32)
        grad_down = jnp.dot(hidden_act.T, expert_grad, preferred_element_type=jnp.float32)
        return total, (grad_gate, grad_up, grad_down)

    start_total = jnp.zeros((TOKENS, D), jnp.float32)
    total, grads = lax.scan(expert_step, start_total,
                            (slot_token, filled, scales, gate_weight, up_weight, down_weight))
    return total.astype(jnp.bfloat16), grads[0], grads[1], grads[2]
```

```python
import functools
import jax
import jax.numpy as jnp
from jax import lax
from jax.experimental import pallas as pl
from jax.experimental.pallas import tpu as pltpu
from jax.sharding import PartitionSpec as P

WINDOW = 32
CAP = 12
BF = jnp.bfloat16
F32 = jnp.float32
MIB = 1024 * 1024


def dot(a, b, ca, cb):
    return lax.dot_general(a, b, (((ca,), (cb,)), ((), ())), preferred_element_type=F32)


def call(kernel, grid, in_specs, out_specs, out_shape, args, scratch=(), grant=24):
    spec = pltpu.PrefetchScalarGridSpec(
        num_scalar_prefetch=1,
        grid=grid,
        in_specs=in_specs,
        out_specs=out_specs,
        scratch_shapes=scratch,
    )
    return pl.pallas_call(
        kernel,
        grid_spec=spec,
        out_shape=out_shape,
        compiler_params=pltpu.CompilerParams(
            dimension_semantics=("arbitrary",) * len(grid), vmem_limit_bytes=grant * MIB
        ),
        cost_estimate=pl.CostEstimate(flops=1, bytes_accessed=1, transcendentals=0),
    )(*args)


def block_codes(ids, gates):
    choices, rows = ids.shape
    expert = lax.broadcasted_iota(jnp.int32, (WINDOW, rows), 0)
    chosen = jnp.zeros((WINDOW, rows), F32)
    gate = jnp.zeros((WINDOW, rows), F32)
    for k in range(choices):
        hit = ids[k : k + 1, :] == expert
        chosen = jnp.where(hit, 1.0, chosen)
        gate = jnp.where(hit, gates[k : k + 1, :], gate)
    earlier = (
        lax.broadcasted_iota(jnp.int32, (rows, rows), 0)
        < lax.broadcasted_iota(jnp.int32, (rows, rows), 1)
    ).astype(F32)
    before = dot(chosen.astype(BF), earlier.astype(BF), 1, 0)
    code = jnp.where(chosen > 0.5, before.astype(jnp.int32), -100)
    return code, gate


def pack_kernel(pos, ids_a, ids_b, gv_a, gv_b, tok_a, tok_b, og_a, og_b, out, sel_t, sel, scale):
    @pl.when(pl.program_id(0) == 0)
    def _():
        core = pos[0]
        code_a, gate_a = block_codes(ids_a[...], gv_a[...])
        code_b, gate_b = block_codes(ids_b[...], gv_b[...])
        code = jnp.concatenate([code_a + CAP * core, code_b + CAP * (1 - core)], axis=1)
        gate = jnp.concatenate([gate_a, gate_b], axis=1)
        width = code.shape[1]
        slot = lax.broadcasted_iota(jnp.int32, (WINDOW, 2 * CAP, width), 1)
        hit = code[:, None, :] == slot
        picked = jnp.where(hit, 1.0, 0.0).reshape(WINDOW * 2 * CAP, width).astype(BF)
        weight = jnp.where(hit, gate[:, None, :], 0.0).reshape(WINDOW * 2 * CAP, width)
        sel[...] = picked
        sel_t[...] = picked.T
        scale[...] = jnp.sum(weight, axis=1, keepdims=True)

    shape = (WINDOW, 2 * CAP, out.shape[3])
    both = jnp.concatenate([tok_a[...], tok_b[...]], axis=0)
    out[:, 0] = dot(sel[...], both, 1, 0).reshape(shape).astype(BF)
    both = jnp.concatenate([og_a[...], og_b[...]], axis=0)
    out[:, 1] = (dot(sel[...], both, 1, 0) * scale[...]).reshape(shape).astype(BF)


def turn_kernel(pos, wd, wg, wu, wd_t, wgu, wgu_t):
    hid = wd.shape[0]
    wd_t[...] = wd[...].T
    wgu[:, :hid] = wg[...]
    wgu[:, hid:] = wu[...]
    wgu_t[:hid] = wg[...].T
    wgu_t[hid:] = wu[...].T


def forward_kernel(pos, x_a, x_b, w_a, w_b, x_t, hidden_t, factors):
    xa, xb = x_a[...], x_b[...]
    pre = dot(xa, w_a[0], 1, 0) + dot(xb, w_b[0], 1, 0)
    hid = pre.shape[1] // 2
    gate_pre, up_pre = pre[:, :hid], pre[:, hid:]
    sig = jax.nn.sigmoid(gate_pre)
    silu = gate_pre * sig
    hidden_t[...] = (silu * up_pre).astype(BF).T
    factors[:, :hid] = up_pre * (sig * (1.0 + gate_pre * (1.0 - sig)))
    factors[:, hid:] = silu
    x_t[pos[0]] = xa.T
    x_t[1 - pos[0]] = xb.T


def act_kernel(pos, g_a, g_b, wd_a, wd_b, factors, backs):
    act = dot(g_a[...], wd_a[0], 1, 0) + dot(g_b[...], wd_b[0], 1, 0)
    hid = act.shape[1]
    backs[:, :hid] = (act * factors[:, :hid]).astype(BF)
    backs[:, hid:] = (act * factors[:, hid:]).astype(BF)


def down_kernel(shift, pos, hidden_t, g_a, g_b, *outs):
    def run(g):
        value = dot(hidden_t[...], g[...], 1, 0)
        step = value.shape[0] // len(outs)
        for i, out in enumerate(outs):
            out[...] = value[i * step : (i + 1) * step].astype(out.dtype)

    mine = (lax.rem(pos[1] + shift, 4) // 2) == pos[0]

    @pl.when(mine)
    def _():
        run(g_a)

    @pl.when(jnp.logical_not(mine))
    def _():
        run(g_b)


def gate_up_kernel(pos, x_t, backs, gate_out, up_out):
    value = dot(x_t[...], backs[...], 1, 0)
    hid = gate_out.shape[1]
    gate_out[...] = value[:, :hid].astype(gate_out.dtype)
    up_out[...] = value[:, hid:].astype(up_out.dtype)


def row_send_kernel(pos, backs, wgu, out):
    out[...] = dot(backs[...], wgu[...], 1, 0).astype(out.dtype)


def row_sum_kernel(pos, backs, wgu, got, out):
    value = dot(backs[...], wgu[...], 1, 0)
    out[...] = (value + got[...].astype(F32)).astype(out.dtype)


def token_kernel(pos, sel, rows, own, other):
    value = dot(sel[...], rows[...], 1, 0)
    half = value.shape[0] // 2
    own[...] = value[:half].astype(BF)
    other[...] = value[half:].astype(BF)


def body(tokens, out_grad, expert_ids, gate_vals, gate_weight, up_weight, down_weight):
    count, features = tokens.shape
    half = features // 2
    quarter = features // 4
    hid = gate_weight.shape[2]
    wide = lax.axis_size("wide")
    choices = expert_ids.shape[1]
    total = WINDOW * 2 * CAP
    core = lax.axis_index("pair").astype(jnp.int32)
    rep = lax.axis_index("rep").astype(jnp.int32)
    pos = jnp.stack([core, rep])
    swap = [(0, 1), (1, 0)]
    up = [(i, (i + 1) % 4) for i in range(4)]
    down = [(i, (i + 3) % 4) for i in range(4)]
    sds = jax.ShapeDtypeStruct

    def full(*shape):
        return pl.BlockSpec(shape, lambda *_: (0,) * len(shape))

    ids = expert_ids.T
    gates = gate_vals.T
    ids_b = lax.ppermute(ids, "pair", swap)
    gv_b = lax.ppermute(gates, "pair", swap)
    tok_b = lax.ppermute(tokens, "pair", swap)
    og_b = lax.ppermute(out_grad, "pair", swap)

    def after(place, *values):
        return lax.optimization_barrier((place, *values))[0]

    steps = 5
    wcol = half // steps
    tok_spec = pl.BlockSpec((count, wcol), lambda i, p: (0, p[0] * steps + i))
    out_col = pl.BlockSpec((total, wcol), lambda i, p: (0, i))
    sent, sel_t = call(
        pack_kernel,
        (steps,),
        [full(choices, count)] * 4 + [tok_spec] * 4,
        [
            pl.BlockSpec((wide, 2, 2 * CAP, wcol), lambda i, p: (0, 0, 0, i)),
            full(2 * count, total),
        ],
        [sds((wide, 2, 2 * CAP, half), BF), sds((2 * count, total), BF)],
        (pos, ids, ids_b, gates, gv_b, tokens, tok_b, out_grad, og_b),
        scratch=[pltpu.VMEM((total, 2 * count), BF), pltpu.VMEM((total, 1), F32)],
        grant=56,
    )
    pos = after(pos, sent)
    wg_full = gate_weight.reshape(features, hid)
    wu_full = up_weight.reshape(features, hid)
    wd = down_weight.reshape(hid, features)
    tall = pl.BlockSpec((features // steps, hid), lambda i, p: (i, 0))
    flat = pl.BlockSpec((hid, features // steps), lambda i, p: (0, i))
    wd_t, wgu, wgu_t = call(
        turn_kernel,
        (steps,),
        [flat, tall, tall],
        [
            tall,
            pl.BlockSpec((features // steps, 2 * hid), lambda i, p: (i, 0)),
            pl.BlockSpec((2 * hid, features // steps), lambda i, p: (0, i)),
        ],
        [sds((features, hid), BF), sds((features, 2 * hid), BF), sds((2 * hid, features), BF)],
        (pos, wd, wg_full, wu_full),
    )
    pos = after(pos, wd_t)
    landed = lax.all_to_all(sent, "wide", split_axis=0, concat_axis=0, tiled=True)
    x_own = landed[:, 0].reshape(total, half)
    g_own = landed[:, 1].reshape(total, half)
    x_oth = lax.ppermute(x_own, "pair", swap)

    parts = 3
    prow = total // parts
    wgu = wgu.reshape(2, half, 2 * hid)
    wd_t = wd_t.reshape(2, half, hid)
    rows_in = pl.BlockSpec((prow, half), lambda i, p: (i, 0))
    rows_two = pl.BlockSpec((prow, 2 * hid), lambda i, p: (i, 0))

    def w_own(n):
        return pl.BlockSpec((1, half, n), lambda i, p: (p[0], 0, 0))

    def w_oth(n):
        return pl.BlockSpec((1, half, n), lambda i, p: (1 - p[0], 0, 0))

    x_t, hidden_t, factors = call(
        forward_kernel,
        (parts,),
        [rows_in, rows_in, w_own(2 * hid), w_oth(2 * hid)],
        [
            pl.BlockSpec((2, half, prow), lambda i, p: (0, 0, i)),
            pl.BlockSpec((hid, prow), lambda i, p: (0, i)),
            rows_two,
        ],
        [sds((2, half, total), BF), sds((hid, total), BF), sds((total, 2 * hid), F32)],
        (pos, x_own, x_oth, wgu, wgu),
    )
    x_t = x_t.reshape(features, total)
    pos = after(pos, hidden_t)
    g_oth = lax.ppermute(g_own, "pair", swap)

    def down_part(place, shift, dtype, pieces):
        g_spec = pl.BlockSpec((total, quarter), lambda i, p: (0, lax.rem(p[1] + shift, 2)))
        return call(
            functools.partial(down_kernel, shift),
            (1,),
            [full(hid, total)] + [g_spec] * 2,
            [full(hid // pieces, quarter)] * pieces,
            [sds((hid // pieces, quarter), dtype)] * pieces,
            (place, hidden_t, g_own, g_oth),
        )

    def gate_up_part(place, shift, dtype):
        return call(
            gate_up_kernel,
            (1,),
            [
                pl.BlockSpec((quarter, total), lambda i, p: (lax.rem(p[1] + shift, 4), 0)),
                full(total, 2 * hid),
            ],
            [full(quarter, hid)] * 2,
            [sds((quarter, hid), dtype)] * 2,
            (place, x_t, backs),
        )

    def add(a, b):
        return (a.astype(F32) + b.astype(F32)).astype(BF)

    far = down_part(pos, 2, BF, 2)
    d_far_u = lax.ppermute(far[0], "rep", up)
    d_far_d = lax.ppermute(far[1], "rep", down)
    pos = after(pos, *far)
    nxt = down_part(pos, 1, BF, 2)
    prv = down_part(pos, 3, BF, 2)
    d_near_u = lax.ppermute(nxt[1], "rep", up)
    d_near_d = lax.ppermute(prv[0], "rep", down)
    pos = after(pos, *nxt, *prv)

    backs = call(
        act_kernel,
        (parts,),
        [rows_in, rows_in, w_own(hid), w_oth(hid), rows_two],
        [rows_two],
        [sds((total, 2 * hid), BF)],
        (pos, g_own, g_oth, wd_t, wd_t, factors),
    )[0]
    d_far_u, d_far_d, backs = lax.optimization_barrier((d_far_u, d_far_d, backs))
    d_sum_u = lax.ppermute(add(nxt[0], d_far_u), "rep", up)
    d_sum_d = lax.ppermute(add(prv[1], d_far_d), "rep", down)

    t_own = pl.BlockSpec((2 * hid, half), lambda i, p: (0, p[0]))
    t_oth = pl.BlockSpec((2 * hid, half), lambda i, p: (0, 1 - p[0]))
    row_send = call(
        row_send_kernel,
        (parts,),
        [rows_two, t_oth],
        [rows_in],
        [sds((total, half), BF)],
        (pos, backs, wgu_t),
    )[0]
    row_got = lax.ppermute(row_send, "pair", swap)
    pos = after(pos, row_send)
    g_far, u_far = gate_up_part(pos, 2, BF)
    pos = after(pos, g_far, u_far)
    row_grad = call(
        row_sum_kernel,
        (parts,),
        [rows_two, t_own, rows_in],
        [rows_in],
        [sds((total, half), BF)],
        (pos, backs, wgu_t, row_got),
    )[0]
    row_grad, pos, g_far, u_far, d_near_u, d_near_d, d_sum_u, d_sum_d = lax.optimization_barrier(
        (row_grad, pos, g_far, u_far, d_near_u, d_near_d, d_sum_u, d_sum_d)
    )
    back = lax.all_to_all(
        row_grad.reshape(wide, 2 * CAP, half), "wide", split_axis=0, concat_axis=0, tiled=True
    ).reshape(total, half)
    g_far = lax.ppermute(g_far, "rep", up)
    u_far = lax.ppermute(u_far, "rep", down)
    g_nxt, u_nxt = gate_up_part(pos, 1, BF)
    g_prv, u_prv = gate_up_part(pos, 3, BF)
    u_near = lax.ppermute(u_nxt, "rep", up)
    g_near = lax.ppermute(g_prv, "rep", down)
    pos = after(pos, g_nxt, u_nxt, g_prv, u_prv)
    g_sum = lax.ppermute(add(g_nxt, g_far), "rep", up)
    u_sum = lax.ppermute(add(u_prv, u_far), "rep", down)

    own_d = down_part(pos, 0, F32, 1)[0]
    own_g, own_u = gate_up_part(pos, 0, F32)

    x_mine, x_other = call(
        token_kernel,
        (steps,),
        [full(2 * count, total), out_col],
        [pl.BlockSpec((count, wcol), lambda i, p: (0, i))] * 2,
        [sds((count, half), BF)] * 2,
        (pos, sel_t, back),
    )
    x_got = lax.ppermute(x_other, "pair", swap)
    first = core == 0
    x_grad = jnp.concatenate(
        [jnp.where(first, x_mine, x_got), jnp.where(first, x_got, x_mine)], axis=1
    )

    gate_grad = own_g + g_sum.astype(F32) + g_near.astype(F32)
    up_grad = own_u + u_sum.astype(F32) + u_near.astype(F32)
    d_low = d_sum_u.astype(F32) + d_near_d.astype(F32)
    d_high = d_near_u.astype(F32) + d_sum_d.astype(F32)
    down_grad = own_d + jnp.concatenate([d_low, d_high], axis=0)
    return (x_grad, gate_grad[None], up_grad[None], down_grad[None])


def solution(mesh):
    rows = P(("pair", "wide", "rep"), None)
    in_specs = (rows, rows, rows, rows) + (
        P("wide", None, "pair"),
        P("wide", None, "pair"),
        P("wide", "pair", None),
    )
    out_specs = (
        rows,
        P("wide", "rep", "pair"),
        P("wide", "rep", "pair"),
        P("wide", "pair", "rep"),
    )
    return jax.shard_map(body, mesh=mesh, in_specs=in_specs, out_specs=out_specs, check_vma=False)
```

```python
import functools
import jax
import jax.numpy as jnp
from jax import lax
from jax.experimental import pallas as pl
from jax.experimental.pallas import tpu as pltpu
from jax.sharding import Mesh, PartitionSpec as P

WINDOW = 32
CAP = 12
BF = jnp.bfloat16
F32 = jnp.float32
MIB = 1024 * 1024


def dot(a, b, ca, cb):
    return lax.dot_general(a, b, (((ca,), (cb,)), ((), ())), preferred_element_type=F32)


def call(kernel, grid, in_specs, out_specs, out_shape, args, scratch=(), grant=24, cost=1):
    spec = pltpu.PrefetchScalarGridSpec(
        num_scalar_prefetch=1,
        grid=grid,
        in_specs=in_specs,
        out_specs=out_specs,
        scratch_shapes=scratch,
    )
    return pl.pallas_call(
        kernel,
        grid_spec=spec,
        out_shape=out_shape,
        compiler_params=pltpu.CompilerParams(
            dimension_semantics=("arbitrary",) * len(grid), vmem_limit_bytes=grant * MIB
        ),
        cost_estimate=pl.CostEstimate(flops=1, bytes_accessed=cost, transcendentals=0),
    )(*args)


def block_codes(ids, gates):
    choices, rows = ids.shape
    expert = lax.broadcasted_iota(jnp.int32, (WINDOW, rows), 0)
    chosen = jnp.zeros((WINDOW, rows), F32)
    gate = jnp.zeros((WINDOW, rows), F32)
    for k in range(choices):
        hit = ids[k : k + 1, :] == expert
        chosen = jnp.where(hit, 1.0, chosen)
        gate = jnp.where(hit, gates[k : k + 1, :], gate)
    earlier = (
        lax.broadcasted_iota(jnp.int32, (rows, rows), 0)
        < lax.broadcasted_iota(jnp.int32, (rows, rows), 1)
    ).astype(F32)
    before = dot(chosen.astype(BF), earlier.astype(BF), 1, 0)
    code = jnp.where(chosen > 0.5, before.astype(jnp.int32), -100)
    return code, gate


def pack_kernel(pos, ids_a, ids_b, gv_a, gv_b, tok_a, tok_b, og_a, og_b, out, keep, give, sel, scale):
    @pl.when(pl.program_id(0) == 0)
    def _():
        core = pos[0]
        code_a, gate_a = block_codes(ids_a[...], gv_a[...])
        code_b, gate_b = block_codes(ids_b[...], gv_b[...])
        code = jnp.concatenate([code_a + CAP * core, code_b + CAP * (1 - core)], axis=1)
        gate = jnp.concatenate([gate_a, gate_b], axis=1)
        width = code.shape[1]
        slot = lax.broadcasted_iota(jnp.int32, (WINDOW, 2 * CAP, width), 1)
        hit = code[:, None, :] == slot
        picked = jnp.where(hit, 1.0, 0.0)
        weight = jnp.where(hit, gate[:, None, :], 0.0).reshape(WINDOW * 2 * CAP, width)
        sel[...] = picked.reshape(WINDOW * 2 * CAP, width).astype(BF)
        split = picked.reshape(WINDOW // 2, 2, 2 * CAP, width)
        even = split[:, 0].reshape(WINDOW * CAP, width).astype(BF).T
        odd = split[:, 1].reshape(WINDOW * CAP, width).astype(BF).T
        keep[...] = jnp.where(pos[2] == 0, even, odd)
        give[...] = jnp.where(pos[2] == 0, odd, even)
        scale[...] = jnp.sum(weight, axis=1, keepdims=True)

    shape = (WINDOW, 2 * CAP, out.shape[3])
    both = jnp.concatenate([tok_a[...], tok_b[...]], axis=0)
    out[:, 0] = dot(sel[...], both, 1, 0).reshape(shape).astype(BF)
    both = jnp.concatenate([og_a[...], og_b[...]], axis=0)
    out[:, 1] = (dot(sel[...], both, 1, 0) * scale[...]).reshape(shape).astype(BF)


def turn_kernel(pos, wd, wg, wu, wd_t, wgu, wgu_t):
    hid = wd.shape[0]
    wd_t[...] = wd[...].T
    wgu[:, :hid] = wg[...]
    wgu[:, hid:] = wu[...]
    wgu_t[:hid] = wg[...].T
    wgu_t[hid:] = wu[...].T


def forward_kernel(pos, x_a, x_b, w_a, w_b, x_t, hidden_t, factors):
    xa, xb = x_a[...], x_b[...]
    pre = dot(xa, w_a[0], 1, 0) + dot(xb, w_b[0], 1, 0)
    hid = pre.shape[1] // 2
    gate_pre, up_pre = pre[:, :hid], pre[:, hid:]
    sig = jax.nn.sigmoid(gate_pre)
    silu = gate_pre * sig
    hidden_t[...] = (silu * up_pre).astype(BF).T
    factors[:, :hid] = up_pre * (sig * (1.0 + gate_pre * (1.0 - sig)))
    factors[:, hid:] = silu
    x_t[pos[0]] = xa.T
    x_t[1 - pos[0]] = xb.T


def act_kernel(pos, g_a, g_b, wd_a, wd_b, factors, backs):
    act = dot(g_a[...], wd_a[0], 1, 0) + dot(g_b[...], wd_b[0], 1, 0)
    hid = act.shape[1]
    backs[:, :hid] = (act * factors[:, :hid]).astype(BF)
    backs[:, hid:] = (act * factors[:, hid:]).astype(BF)


def down_kernel(shift, pos, hidden_t, g_a, g_b, *outs):
    def run(g):
        value = dot(hidden_t[...], g[...], 1, 0)
        step = value.shape[0] // len(outs)
        for i, out in enumerate(outs):
            out[...] = value[i * step : (i + 1) * step].astype(out.dtype)

    mine = (lax.rem(pos[1] + shift, 4) // 2) == pos[0]

    @pl.when(mine)
    def _():
        run(g_a)

    @pl.when(jnp.logical_not(mine))
    def _():
        run(g_b)


def gate_up_kernel(pos, x_t, backs, gate_out, up_out):
    value = dot(x_t[...], backs[...], 1, 0)
    hid = gate_out.shape[1]
    gate_out[...] = value[:, :hid].astype(gate_out.dtype)
    up_out[...] = value[:, hid:].astype(up_out.dtype)


def row_send_kernel(pos, backs, wgu, out):
    out[...] = dot(backs[...], wgu[...], 1, 0).astype(out.dtype)


def row_sum_kernel(pos, backs, wgu, got, out):
    value = dot(backs[...], wgu[...], 1, 0)
    out[...] = (value + got[...].astype(F32)).astype(out.dtype)


def token_kernel(pos, keep, got, rows_keep, rows_got, own, other):
    for sel, rows, out in ((keep, rows_keep, own), (got, rows_got, other)):
        n, _, slots, m = rows.shape
        flat = rows[:, 0].astype(F32).reshape(n * slots, m).astype(BF)
        out[...] = dot(sel[...], flat, 1, 0).astype(BF)


def body(tokens, out_grad, expert_ids, gate_vals, gate_weight, up_weight, down_weight):
    count, features = tokens.shape
    half = features // 2
    quarter = features // 4
    hid = gate_weight.shape[2]
    plane = ("y", "x")
    experts = ("y", "x", "zlo")
    wide = lax.axis_size(experts)
    choices = expert_ids.shape[1]
    total = WINDOW * 2 * CAP
    core = lax.axis_index("pair").astype(jnp.int32)
    rep = lax.axis_index("rep").astype(jnp.int32)
    parity = lax.axis_index("zlo").astype(jnp.int32)
    pos = jnp.stack([core, rep, parity])
    swap = [(0, 1), (1, 0)]
    up = [(i, (i + 1) % 4) for i in range(4)]
    down = [(i, (i + 3) % 4) for i in range(4)]
    sds = jax.ShapeDtypeStruct

    def full(*shape):
        return pl.BlockSpec(shape, lambda *_: (0,) * len(shape))

    ids = expert_ids.T
    gates = gate_vals.T
    ids_b = lax.ppermute(ids, "pair", swap)
    gv_b = lax.ppermute(gates, "pair", swap)
    tok_b = lax.ppermute(tokens, "pair", swap)
    og_b = lax.ppermute(out_grad, "pair", swap)

    def after(place, *values):
        return lax.optimization_barrier((place, *values))[0]

    steps = 5
    wcol = half // steps
    tok_spec = pl.BlockSpec((count, wcol), lambda i, p: (0, p[0] * steps + i))
    out_col = pl.BlockSpec((total, wcol), lambda i, p: (0, i))
    sent, keep, give = call(
        pack_kernel,
        (steps,),
        [full(choices, count)] * 4 + [tok_spec] * 4,
        [
            pl.BlockSpec((wide, 2, 2 * CAP, wcol), lambda i, p: (0, 0, 0, i)),
            full(2 * count, total // 2),
            full(2 * count, total // 2),
        ],
        [sds((wide, 2, 2 * CAP, half), BF)] + [sds((2 * count, total // 2), BF)] * 2,
        (pos, ids, ids_b, gates, gv_b, tokens, tok_b, out_grad, og_b),
        scratch=[pltpu.VMEM((total, 2 * count), BF), pltpu.VMEM((total, 1), F32)],
        grant=56,
    )
    pos = after(pos, sent)
    wg_full = gate_weight.reshape(features, hid)
    wu_full = up_weight.reshape(features, hid)
    wd = down_weight.reshape(hid, features)
    tall = pl.BlockSpec((features // steps, hid), lambda i, p: (i, 0))
    flat = pl.BlockSpec((hid, features // steps), lambda i, p: (0, i))
    wd_t, wgu, wgu_t = call(
        turn_kernel,
        (steps,),
        [flat, tall, tall],
        [
            tall,
            pl.BlockSpec((features // steps, 2 * hid), lambda i, p: (i, 0)),
            pl.BlockSpec((2 * hid, features // steps), lambda i, p: (0, i)),
        ],
        [sds((features, hid), BF), sds((features, 2 * hid), BF), sds((2 * hid, features), BF)],
        (pos, wd, wg_full, wu_full),
    )
    pos = after(pos, wd_t)
    landed = lax.all_to_all(sent, experts, split_axis=0, concat_axis=0, tiled=True)
    x_own = landed[:, 0].reshape(total, half)
    g_own = landed[:, 1].reshape(total, half)
    got = lax.ppermute(give, "zlo", swap)
    x_oth = lax.ppermute(x_own, "pair", swap)

    parts = 3
    prow = total // parts
    wgu = wgu.reshape(2, half, 2 * hid)
    wd_t = wd_t.reshape(2, half, hid)
    rows_in = pl.BlockSpec((prow, half), lambda i, p: (i, 0))
    rows_two = pl.BlockSpec((prow, 2 * hid), lambda i, p: (i, 0))

    def w_own(n):
        return pl.BlockSpec((1, half, n), lambda i, p: (p[0], 0, 0))

    def w_oth(n):
        return pl.BlockSpec((1, half, n), lambda i, p: (1 - p[0], 0, 0))

    x_t, hidden_t, factors = call(
        forward_kernel,
        (parts,),
        [rows_in, rows_in, w_own(2 * hid), w_oth(2 * hid)],
        [
            pl.BlockSpec((2, half, prow), lambda i, p: (0, 0, i)),
            pl.BlockSpec((hid, prow), lambda i, p: (0, i)),
            rows_two,
        ],
        [sds((2, half, total), BF), sds((hid, total), BF), sds((total, 2 * hid), F32)],
        (pos, x_own, x_oth, wgu, wgu),
    )
    x_t = x_t.reshape(features, total)
    pos = after(pos, hidden_t, got)
    g_oth = lax.ppermute(g_own, "pair", swap)

    def down_part(place, shift, dtype, pieces):
        g_spec = pl.BlockSpec((total, quarter), lambda i, p: (0, lax.rem(p[1] + shift, 2)))
        return call(
            functools.partial(down_kernel, shift),
            (1,),
            [full(hid, total)] + [g_spec] * 2,
            [full(hid // pieces, quarter)] * pieces,
            [sds((hid // pieces, quarter), dtype)] * pieces,
            (place, hidden_t, g_own, g_oth),
        )

    def gate_up_part(place, shift, dtype):
        return call(
            gate_up_kernel,
            (1,),
            [
                pl.BlockSpec((quarter, total), lambda i, p: (lax.rem(p[1] + shift, 4), 0)),
                full(total, 2 * hid),
            ],
            [full(quarter, hid)] * 2,
            [sds((quarter, hid), dtype)] * 2,
            (place, x_t, backs),
        )

    def add(a, b):
        return (a.astype(F32) + b.astype(F32)).astype(BF)

    far = down_part(pos, 2, BF, 2)
    d_far_u = lax.ppermute(far[0], "rep", up)
    d_far_d = lax.ppermute(far[1], "rep", down)
    pos = after(pos, *far)
    nxt = down_part(pos, 1, BF, 2)
    prv = down_part(pos, 3, BF, 2)
    d_near_u = lax.ppermute(nxt[1], "rep", up)
    d_near_d = lax.ppermute(prv[0], "rep", down)
    pos = after(pos, *nxt, *prv)

    backs = call(
        act_kernel,
        (parts,),
        [rows_in, rows_in, w_own(hid), w_oth(hid), rows_two],
        [rows_two],
        [sds((total, 2 * hid), BF)],
        (pos, g_own, g_oth, wd_t, wd_t, factors),
    )[0]
    d_far_u, d_far_d, backs = lax.optimization_barrier((d_far_u, d_far_d, backs))
    d_sum_u = lax.ppermute(add(nxt[0], d_far_u), "rep", up)
    d_sum_d = lax.ppermute(add(prv[1], d_far_d), "rep", down)

    t_own = pl.BlockSpec((2 * hid, half), lambda i, p: (0, p[0]))
    t_oth = pl.BlockSpec((2 * hid, half), lambda i, p: (0, 1 - p[0]))
    row_send = call(
        row_send_kernel,
        (parts,),
        [rows_two, t_oth],
        [rows_in],
        [sds((total, half), BF)],
        (pos, backs, wgu_t),
    )[0]
    row_got = lax.ppermute(row_send, "pair", swap)
    pos = after(pos, row_send)
    g_far, u_far = gate_up_part(pos, 2, BF)
    pos = after(pos, g_far, u_far)
    row_grad = call(
        row_sum_kernel,
        (parts,),
        [rows_two, t_own, rows_in],
        [rows_in],
        [sds((total, half), BF)],
        (pos, backs, wgu_t, row_got),
    )[0]
    row_grad, pos, g_far, u_far, d_near_u, d_near_d, d_sum_u, d_sum_d = lax.optimization_barrier(
        (row_grad, pos, g_far, u_far, d_near_u, d_near_d, d_sum_u, d_sum_d)
    )
    nodes = wide // 2
    back = lax.all_to_all(
        row_grad.reshape(nodes, 4 * CAP, half), plane, split_axis=0, concat_axis=0, tiled=True
    ).reshape(nodes, 2, 2 * CAP, half)
    g_far = lax.ppermute(g_far, "rep", up)
    u_far = lax.ppermute(u_far, "rep", down)
    g_nxt, u_nxt = gate_up_part(pos, 1, BF)
    g_prv, u_prv = gate_up_part(pos, 3, BF)
    u_near = lax.ppermute(u_nxt, "rep", up)
    g_near = lax.ppermute(g_prv, "rep", down)
    pos = after(pos, g_nxt, u_nxt, g_prv, u_prv)
    x_near, x_far = call(
        token_kernel,
        (steps,),
        [
            full(2 * count, total // 2),
            full(2 * count, total // 2),
            pl.BlockSpec((nodes, 1, 2 * CAP, wcol), lambda i, p: (0, p[2], 0, i)),
            pl.BlockSpec((nodes, 1, 2 * CAP, wcol), lambda i, p: (0, 1 - p[2], 0, i)),
        ],
        [pl.BlockSpec((2 * count, wcol), lambda i, p: (0, i))] * 2,
        [sds((2 * count, half), BF)] * 2,
        (pos, keep, got, back, back),
    )
    g_far, u_far, x_far = lax.optimization_barrier((g_far, u_far, x_far))
    x_far = lax.ppermute(x_far, "zlo", swap)
    g_sum = lax.ppermute(add(g_nxt, g_far), "rep", up)
    u_sum = lax.ppermute(add(u_prv, u_far), "rep", down)

    own_d = down_part(pos, 0, F32, 1)[0]
    own_g, own_u = gate_up_part(pos, 0, F32)

    x_both = (x_near.astype(F32) + x_far.astype(F32)).astype(BF)
    x_mine, x_other = x_both[:count], x_both[count:]
    x_got = lax.ppermute(x_other, "pair", swap)
    first = core == 0
    x_grad = jnp.concatenate(
        [jnp.where(first, x_mine, x_got), jnp.where(first, x_got, x_mine)], axis=1
    )

    gate_grad = own_g + g_sum.astype(F32) + g_near.astype(F32)
    up_grad = own_u + u_sum.astype(F32) + u_near.astype(F32)
    d_low = d_sum_u.astype(F32) + d_near_d.astype(F32)
    d_high = d_near_u.astype(F32) + d_sum_d.astype(F32)
    down_grad = own_d + jnp.concatenate([d_low, d_high], axis=0)
    return (x_grad, gate_grad[None], up_grad[None], down_grad[None])


def solution(mesh):
    axes = ("pair", "y", "x", "zlo", "rep")
    pairs, wide, reps = mesh.devices.shape
    cut = Mesh(mesh.devices.reshape(pairs, 4, wide // 8, 2, reps), axes)
    rows = P(axes, None)
    experts = ("y", "x", "zlo")
    in_specs = (rows, rows, rows, rows) + (
        P(experts, None, "pair"),
        P(experts, None, "pair"),
        P(experts, "pair", None),
    )
    out_specs = (
        rows,
        P(experts, "rep", "pair"),
        P(experts, "rep", "pair"),
        P(experts, "pair", "rep"),
    )
    return jax.shard_map(body, mesh=cut, in_specs=in_specs, out_specs=out_specs, check_vma=False)
```

```python
import functools
import jax
import jax.numpy as jnp
from jax import lax
from jax.experimental import pallas as pl
from jax.experimental.pallas import tpu as pltpu
from jax.sharding import Mesh, PartitionSpec as P

WINDOW = 32
CAP = 12
BF = jnp.bfloat16
F32 = jnp.float32
MIB = 1024 * 1024


def dot(a, b, ca, cb):
    return lax.dot_general(a, b, (((ca,), (cb,)), ((), ())), preferred_element_type=F32)


def call(kernel, grid, in_specs, out_specs, out_shape, args, scratch=(), grant=24, cost=1):
    spec = pltpu.PrefetchScalarGridSpec(
        num_scalar_prefetch=1,
        grid=grid,
        in_specs=in_specs,
        out_specs=out_specs,
        scratch_shapes=scratch,
    )
    return pl.pallas_call(
        kernel,
        grid_spec=spec,
        out_shape=out_shape,
        compiler_params=pltpu.CompilerParams(
            dimension_semantics=("arbitrary",) * len(grid), vmem_limit_bytes=grant * MIB
        ),
        cost_estimate=pl.CostEstimate(flops=1, bytes_accessed=cost, transcendentals=0),
    )(*args)


def block_codes(ids, gates):
    choices, rows = ids.shape
    expert = lax.broadcasted_iota(jnp.int32, (WINDOW, rows), 0)
    chosen = jnp.zeros((WINDOW, rows), F32)
    gate = jnp.zeros((WINDOW, rows), F32)
    for k in range(choices):
        hit = ids[k : k + 1, :] == expert
        chosen = jnp.where(hit, 1.0, chosen)
        gate = jnp.where(hit, gates[k : k + 1, :], gate)
    earlier = (
        lax.broadcasted_iota(jnp.int32, (rows, rows), 0)
        < lax.broadcasted_iota(jnp.int32, (rows, rows), 1)
    ).astype(F32)
    before = dot(chosen.astype(BF), earlier.astype(BF), 1, 0)
    code = jnp.where(chosen > 0.5, before.astype(jnp.int32), -100)
    return code, gate


def pack_kernel(pos, ids_a, ids_b, gv_a, gv_b, tok_a, tok_b, og_a, og_b, out, keep, give, sel, scale):
    @pl.when(pl.program_id(0) == 0)
    def _():
        core = pos[0]
        code_a, gate_a = block_codes(ids_a[...], gv_a[...])
        code_b, gate_b = block_codes(ids_b[...], gv_b[...])
        code = jnp.concatenate([code_a + CAP * core, code_b + CAP * (1 - core)], axis=1)
        gate = jnp.concatenate([gate_a, gate_b], axis=1)
        width = code.shape[1]
        slot = lax.broadcasted_iota(jnp.int32, (WINDOW, 2 * CAP, width), 1)
        hit = code[:, None, :] == slot
        picked = jnp.where(hit, 1.0, 0.0)
        weight = jnp.where(hit, gate[:, None, :], 0.0).reshape(WINDOW * 2 * CAP, width)
        sel[...] = picked.reshape(WINDOW * 2 * CAP, width).astype(BF)
        split = picked.reshape(WINDOW // 2, 2, 2 * CAP, width)
        even = split[:, 0].reshape(WINDOW * CAP, width).astype(BF).T
        odd = split[:, 1].reshape(WINDOW * CAP, width).astype(BF).T
        keep[...] = jnp.where(pos[2] == 0, even, odd)
        give[...] = jnp.where(pos[2] == 0, odd, even)
        scale[...] = jnp.sum(weight, axis=1, keepdims=True)

    shape = (WINDOW, 2 * CAP, out.shape[3])
    both = jnp.concatenate([tok_a[...], tok_b[...]], axis=0)
    out[:, 0] = dot(sel[...], both, 1, 0).reshape(shape).astype(BF)
    both = jnp.concatenate([og_a[...], og_b[...]], axis=0)
    out[:, 1] = (dot(sel[...], both, 1, 0) * scale[...]).reshape(shape).astype(BF)


def turn_kernel(pos, wd, wg, wu, wd_t, wgu, wgu_t):
    hid = wd.shape[0]
    wd_t[...] = wd[...].T
    wgu[:, :hid] = wg[...]
    wgu[:, hid:] = wu[...]
    wgu_t[:hid] = wg[...].T
    wgu_t[hid:] = wu[...].T


def forward_kernel(pos, x_a, x_b, w_a, w_b, x_t, hidden_t, factors):
    xa, xb = x_a[...], x_b[...]
    pre = dot(xa, w_a[0], 1, 0) + dot(xb, w_b[0], 1, 0)
    hid = pre.shape[1] // 2
    gate_pre, up_pre = pre[:, :hid], pre[:, hid:]
    sig = jax.nn.sigmoid(gate_pre)
    silu = gate_pre * sig
    hidden_t[...] = (silu * up_pre).astype(BF).T
    factors[:, :hid] = up_pre * (sig * (1.0 + gate_pre * (1.0 - sig)))
    factors[:, hid:] = silu
    x_t[pos[0]] = xa.T
    x_t[1 - pos[0]] = xb.T


def act_kernel(pos, g_a, g_b, wd_a, wd_b, factors, backs):
    act = dot(g_a[...], wd_a[0], 1, 0) + dot(g_b[...], wd_b[0], 1, 0)
    hid = act.shape[1]
    backs[:, :hid] = (act * factors[:, :hid]).astype(BF)
    backs[:, hid:] = (act * factors[:, hid:]).astype(BF)


def down_kernel(shift, pos, hidden_t, g_a, g_b, *outs):
    def run(g):
        value = dot(hidden_t[...], g[...], 1, 0)
        step = value.shape[0] // len(outs)
        for i, out in enumerate(outs):
            out[...] = value[i * step : (i + 1) * step].astype(out.dtype)

    mine = (lax.rem(pos[1] + shift, 4) // 2) == pos[0]

    @pl.when(mine)
    def _():
        run(g_a)

    @pl.when(jnp.logical_not(mine))
    def _():
        run(g_b)


def gate_up_kernel(pos, x_t, backs, gate_out, up_out):
    value = dot(x_t[...], backs[...], 1, 0)
    hid = gate_out.shape[1]
    gate_out[...] = value[:, :hid].astype(gate_out.dtype)
    up_out[...] = value[:, hid:].astype(up_out.dtype)


def row_send_kernel(pos, backs, wgu, out):
    out[...] = dot(backs[...], wgu[...], 1, 0).astype(out.dtype)


def row_sum_kernel(pos, backs, wgu, got, out):
    value = dot(backs[...], wgu[...], 1, 0)
    out[...] = (value + got[...].astype(F32)).astype(out.dtype)


def token_kernel(pos, keep, got, rows_keep, rows_got, own, other):
    for sel, rows, out in ((keep, rows_keep, own), (got, rows_got, other)):
        n, _, slots, m = rows.shape
        flat = rows[:, 0].astype(F32).reshape(n * slots, m).astype(BF)
        out[...] = dot(sel[...], flat, 1, 0).astype(BF)


def body(tokens, out_grad, expert_ids, gate_vals, gate_weight, up_weight, down_weight):
    count, features = tokens.shape
    half = features // 2
    quarter = features // 4
    hid = gate_weight.shape[2]
    plane = ("y", "x")
    experts = ("y", "x", "zlo")
    wide = lax.axis_size(experts)
    choices = expert_ids.shape[1]
    total = WINDOW * 2 * CAP
    core = lax.axis_index("pair").astype(jnp.int32)
    rep = lax.axis_index("rep").astype(jnp.int32)
    parity = lax.axis_index("zlo").astype(jnp.int32)
    pos = jnp.stack([core, rep, parity])
    swap = [(0, 1), (1, 0)]
    up = [(i, (i + 1) % 4) for i in range(4)]
    down = [(i, (i + 3) % 4) for i in range(4)]
    sds = jax.ShapeDtypeStruct

    def full(*shape):
        return pl.BlockSpec(shape, lambda *_: (0,) * len(shape))

    ids = expert_ids.T
    gates = gate_vals.T
    ids_b = lax.ppermute(ids, "pair", swap)
    gv_b = lax.ppermute(gates, "pair", swap)
    tok_b = lax.ppermute(tokens, "pair", swap)
    og_b = lax.ppermute(out_grad, "pair", swap)

    def after(place, *values):
        return lax.optimization_barrier((place, *values))[0]

    steps = 5
    sent, keep, give = call(
        pack_kernel,
        (1,),
        [full(choices, count)] * 4 + [pl.BlockSpec((count, half // 1), lambda i, p: (0, p[0] * 1 + i))] * 4,
        [
            pl.BlockSpec((wide, 2, 2 * CAP, half // 1), lambda i, p: (0, 0, 0, i)),
            full(2 * count, total // 2),
            full(2 * count, total // 2),
        ],
        [sds((wide, 2, 2 * CAP, half), BF)] + [sds((2 * count, total // 2), BF)] * 2,
        (pos, ids, ids_b, gates, gv_b, tokens, tok_b, out_grad, og_b),
        scratch=[pltpu.VMEM((total, 2 * count), BF), pltpu.VMEM((total, 1), F32)],
        grant=56,
    )
    pos = after(pos, sent)
    wg_full = gate_weight.reshape(features, hid)
    wu_full = up_weight.reshape(features, hid)
    wd = down_weight.reshape(hid, features)
    tall = pl.BlockSpec((features // steps, hid), lambda i, p: (i, 0))
    flat = pl.BlockSpec((hid, features // steps), lambda i, p: (0, i))
    wd_t, wgu, wgu_t = call(
        turn_kernel,
        (steps,),
        [flat, tall, tall],
        [
            tall,
            pl.BlockSpec((features // steps, 2 * hid), lambda i, p: (i, 0)),
            pl.BlockSpec((2 * hid, features // steps), lambda i, p: (0, i)),
        ],
        [sds((features, hid), BF), sds((features, 2 * hid), BF), sds((2 * hid, features), BF)],
        (pos, wd, wg_full, wu_full),
    )
    pos = after(pos, wd_t)
    landed = lax.all_to_all(sent, experts, split_axis=0, concat_axis=0, tiled=True)
    x_own = landed[:, 0].reshape(total, half)
    g_own = landed[:, 1].reshape(total, half)
    got = lax.ppermute(give, "zlo", swap)
    x_oth = lax.ppermute(x_own, "pair", swap)

    parts = 3
    prow = total // parts
    wgu = wgu.reshape(2, half, 2 * hid)
    wd_t = wd_t.reshape(2, half, hid)
    rows_in = pl.BlockSpec((prow, half), lambda i, p: (i, 0))
    rows_two = pl.BlockSpec((prow, 2 * hid), lambda i, p: (i, 0))

    def w_own(n):
        return pl.BlockSpec((1, half, n), lambda i, p: (p[0], 0, 0))

    def w_oth(n):
        return pl.BlockSpec((1, half, n), lambda i, p: (1 - p[0], 0, 0))

    x_t, hidden_t, factors = call(
        forward_kernel,
        (parts,),
        [rows_in, rows_in, w_own(2 * hid), w_oth(2 * hid)],
        [
            pl.BlockSpec((2, half, prow), lambda i, p: (0, 0, i)),
            pl.BlockSpec((hid, prow), lambda i, p: (0, i)),
            rows_two,
        ],
        [sds((2, half, total), BF), sds((hid, total), BF), sds((total, 2 * hid), F32)],
        (pos, x_own, x_oth, wgu, wgu),
    )
    x_t = x_t.reshape(features, total)
    pos = after(pos, hidden_t, got)
    g_oth = lax.ppermute(g_own, "pair", swap)

    def down_part(place, shift, dtype, pieces):
        g_spec = pl.BlockSpec((total, quarter), lambda i, p: (0, lax.rem(p[1] + shift, 2)))
        return call(
            functools.partial(down_kernel, shift),
            (1,),
            [full(hid, total)] + [g_spec] * 2,
            [full(hid // pieces, quarter)] * pieces,
            [sds((hid // pieces, quarter), dtype)] * pieces,
            (place, hidden_t, g_own, g_oth),
        )

    def gate_up_part(place, shift, dtype):
        return call(
            gate_up_kernel,
            (1,),
            [
                pl.BlockSpec((quarter, total), lambda i, p: (lax.rem(p[1] + shift, 4), 0)),
                full(total, 2 * hid),
            ],
            [full(quarter, hid)] * 2,
            [sds((quarter, hid), dtype)] * 2,
            (place, x_t, backs),
        )

    def add(a, b):
        return (a.astype(F32) + b.astype(F32)).astype(BF)

    far = down_part(pos, 2, BF, 2)
    d_far_u = lax.ppermute(far[0], "rep", up)
    d_far_d = lax.ppermute(far[1], "rep", down)
    pos = after(pos, *far)
    nxt = down_part(pos, 1, BF, 2)
    prv = down_part(pos, 3, BF, 2)
    d_near_u = lax.ppermute(nxt[1], "rep", up)
    d_near_d = lax.ppermute(prv[0], "rep", down)
    pos = after(pos, *nxt, *prv)

    backs = call(
        act_kernel,
        (parts,),
        [rows_in, rows_in, w_own(hid), w_oth(hid), rows_two],
        [rows_two],
        [sds((total, 2 * hid), BF)],
        (pos, g_own, g_oth, wd_t, wd_t, factors),
    )[0]
    d_far_u, d_far_d, backs = lax.optimization_barrier((d_far_u, d_far_d, backs))
    d_sum_u = lax.ppermute(add(nxt[0], d_far_u), "rep", up)
    d_sum_d = lax.ppermute(add(prv[1], d_far_d), "rep", down)

    t_own = pl.BlockSpec((2 * hid, half), lambda i, p: (0, p[0]))
    t_oth = pl.BlockSpec((2 * hid, half), lambda i, p: (0, 1 - p[0]))
    row_send = call(
        row_send_kernel,
        (parts,),
        [rows_two, t_oth],
        [rows_in],
        [sds((total, half), BF)],
        (pos, backs, wgu_t),
    )[0]
    row_got = lax.ppermute(row_send, "pair", swap)
    pos = after(pos, row_send)
    g_far, u_far = gate_up_part(pos, 2, BF)
    pos = after(pos, g_far, u_far)
    row_grad = call(
        row_sum_kernel,
        (parts,),
        [rows_two, t_own, rows_in],
        [rows_in],
        [sds((total, half), BF)],
        (pos, backs, wgu_t, row_got),
    )[0]
    row_grad, pos, g_far, u_far, d_near_u, d_near_d, d_sum_u, d_sum_d = lax.optimization_barrier(
        (row_grad, pos, g_far, u_far, d_near_u, d_near_d, d_sum_u, d_sum_d)
    )
    nodes = wide // 2
    back = lax.all_to_all(
        row_grad.reshape(nodes, 4 * CAP, half), plane, split_axis=0, concat_axis=0, tiled=True
    ).reshape(nodes, 2, 2 * CAP, half)
    g_far = lax.ppermute(g_far, "rep", up)
    u_far = lax.ppermute(u_far, "rep", down)
    g_nxt, u_nxt = gate_up_part(pos, 1, BF)
    g_prv, u_prv = gate_up_part(pos, 3, BF)
    u_near = lax.ppermute(u_nxt, "rep", up)
    g_near = lax.ppermute(g_prv, "rep", down)
    pos = after(pos, g_nxt, u_nxt, g_prv, u_prv)
    x_near, x_far = call(
        token_kernel,
        (2,),
        [
            full(2 * count, total // 2),
            full(2 * count, total // 2),
            pl.BlockSpec((nodes, 1, 2 * CAP, half // 2), lambda i, p: (0, p[2], 0, i)),
            pl.BlockSpec((nodes, 1, 2 * CAP, half // 2), lambda i, p: (0, 1 - p[2], 0, i)),
        ],
        [pl.BlockSpec((2 * count, half // 2), lambda i, p: (0, i))] * 2,
        [sds((2 * count, half), BF)] * 2,
        (pos, keep, got, back, back),
    )
    g_far, u_far, x_far = lax.optimization_barrier((g_far, u_far, x_far))
    x_far = lax.ppermute(x_far, "zlo", swap)
    g_sum = lax.ppermute(add(g_nxt, g_far), "rep", up)
    u_sum = lax.ppermute(add(u_prv, u_far), "rep", down)

    own_d = down_part(pos, 0, F32, 1)[0]
    own_g, own_u = gate_up_part(pos, 0, F32)

    x_both = (x_near.astype(F32) + x_far.astype(F32)).astype(BF)
    x_mine, x_other = x_both[:count], x_both[count:]
    x_got = lax.ppermute(x_other, "pair", swap)
    first = core == 0
    x_grad = jnp.concatenate(
        [jnp.where(first, x_mine, x_got), jnp.where(first, x_got, x_mine)], axis=1
    )

    gate_grad = own_g + g_sum.astype(F32) + g_near.astype(F32)
    up_grad = own_u + u_sum.astype(F32) + u_near.astype(F32)
    d_low = d_sum_u.astype(F32) + d_near_d.astype(F32)
    d_high = d_near_u.astype(F32) + d_sum_d.astype(F32)
    down_grad = own_d + jnp.concatenate([d_low, d_high], axis=0)
    return (x_grad, gate_grad[None], up_grad[None], down_grad[None])


def solution(mesh):
    axes = ("pair", "y", "x", "zlo", "rep")
    pairs, wide, reps = mesh.devices.shape
    cut = Mesh(mesh.devices.reshape(pairs, 4, wide // 8, 2, reps), axes)
    rows = P(axes, None)
    experts = ("y", "x", "zlo")
    in_specs = (rows, rows, rows, rows) + (
        P(experts, None, "pair"),
        P(experts, None, "pair"),
        P(experts, "pair", None),
    )
    out_specs = (
        rows,
        P(experts, "rep", "pair"),
        P(experts, "rep", "pair"),
        P(experts, "pair", "rep"),
    )
    return jax.shard_map(body, mesh=cut, in_specs=in_specs, out_specs=out_specs, check_vma=False)
```
